32 devices in a mesh: ctx: 8 (over z, x), head: 4 (over y, core).
Axes of the slice: x: 2, y: 2, z: 4, core: 2. Of those that a mesh axis runs over, the one named last changes fastest.
Arguments:
- signal: bfloat16 [8192, 8192], P('ctx', 'head'), may hold values from -6 to 6
- step_size: float32 [128, 8192], P('head', 'ctx'), may hold values from 0.005 to 0.05
- log_decay: float32 [128, 8192], P('head', 'ctx'), may hold values from -0.7 to 0, as said below
- input_map: bfloat16 [8192, 1024], P('ctx', 'head'), may hold values from -1.75 to 1.75
- output_map: bfloat16 [8192, 1024], P('ctx', 'head'), may hold values from -1.75 to 1.75
- skip_gain: float32 [128], P('head'), may hold values from 0.5 to 2
- grad_out: bfloat16 [8192, 8192], P('ctx', 'head'), may hold values from -18 to 18
Outputs:
- grad_signal: bfloat16 [8192, 8192], P('ctx', 'head')
- grad_step: float32 [128, 8192], P('head', 'ctx')
- grad_decay: float32 [128, 8192], P('head', 'ctx')
- grad_input_map: bfloat16 [8192, 1024], P('ctx', 'head')
- grad_output_map: bfloat16 [8192, 1024], P('ctx', 'head')
- grad_skip: float32 [128], P('head')
The draws below stay inside these ranges and needn't reach their ends.
Inputs may be any that keep to these rules, and one draw needn't show every extreme that they name: `log_decay`: log-decays of the state, never positive.
All inputs are finite; a program needn't handle non-finite values.
Results may differ from the reference program's by a relative error of at most 0.001.
Values sent between devices are 32-bit elements; how exact they have to be, the bound alone decides.
A program may use at most 192 MiB of HBM per device.

```python
import math
import jax
import jax.numpy as jnp
from jax import lax

SSM_HEAD_TOTAL = 128
P_SIZE = 64
N = 128
G = 8
BLOCK = 256
TOK_DEV = 1024
SEQUENCE_SPAN = 8192


def draw_log_decay(key, part):
    parallel_tracks = jax.random.split(key, 7)
    share = 0.5
    slow_heads = jax.random.uniform(parallel_tracks[0], (SSM_HEAD_TOTAL, 1), jnp.float32) < share
    slow_rate = jnp.exp(jax.random.uniform(parallel_tracks[1], (SSM_HEAD_TOTAL, 1), jnp.float32, math.log(0.1), math.log(0.6))) / SEQUENCE_SPAN
    fast_rate = jnp.exp(jax.random.uniform(parallel_tracks[2], (SSM_HEAD_TOTAL, 1), jnp.float32, math.log(1.0 / 50.0), math.log(1.0 / 30.0)))
    rough = jnp.exp(jax.random.uniform(parallel_tracks[3], (SSM_HEAD_TOTAL, SEQUENCE_SPAN), jnp.float32, math.log(0.5), math.log(2.0)))
    block_factor = jnp.exp(jax.random.uniform(parallel_tracks[4], (SSM_HEAD_TOTAL, SEQUENCE_SPAN // TOK_DEV), jnp.float32, math.log(0.5), math.log(2.0)))
    block_factor = jnp.repeat(block_factor, TOK_DEV, axis=1)
    starting_index = jnp.where(slow_heads, slow_rate, fast_rate) * rough * block_factor
    batched_clusters = jax.random.uniform(parallel_tracks[5], (SSM_HEAD_TOTAL, SEQUENCE_SPAN), jnp.float32) < 2.0 / SEQUENCE_SPAN
    recurrence_levels = jax.random.uniform(parallel_tracks[6], (SSM_HEAD_TOTAL, SEQUENCE_SPAN), jnp.float32, 0.2, 0.4)
    entry_lines = -starting_index + jnp.where(batched_clusters, jnp.log1p(-recurrence_levels), 0.0)
    return entry_lines.astype(jnp.float32)


def draw_grad_out(key, part):
    positions = jnp.arange(SEQUENCE_SPAN, dtype=jnp.float32)[:, None] / (SEQUENCE_SPAN - 1)
    entry_lines = jnp.clip(jax.random.normal(key, (SEQUENCE_SPAN, SSM_HEAD_TOTAL * P_SIZE), jnp.float32), -6.0, 6.0) * jnp.exp(positions * math.log(3.0))
    return entry_lines.astype(jnp.bfloat16)


def block_scale(stream_key, dims, cuts, smallest, high):
    loudness, own = 1.0, jax.random.fold_in(stream_key, 6)
    for position, shards_of in cuts:
        draws = jnp.exp(jax.random.uniform(jax.random.fold_in(own, position), (shards_of,), jnp.float32, smallest / len(cuts), high / len(cuts)))
        loudness = loudness * jnp.repeat(draws, dims[position] // shards_of).reshape([-1 if axis == position else 1 for axis in range(len(dims))])
    return loudness


def bell_draw(own_key, dims, scale, limit, cuts=(), kind=jnp.bfloat16):
    values = scale * jax.random.normal(own_key, dims, jnp.float32)
    if cuts:
        values = values * block_scale(own_key, dims, cuts, -0.22, 0.18)
    return jnp.clip(values, -limit, limit).astype(kind)


def setup_inputs(seed: int = 0) -> dict:
    splits = jax.random.split(jax.random.key(seed), 8)
    signal = bell_draw(splits[0], (SEQUENCE_SPAN, SSM_HEAD_TOTAL * P_SIZE), 1.0, 6.0, ((0, 8), (1, 4)))
    step_size = jnp.clip(jnp.exp(math.log(0.05) - 2.3025851 * jax.random.uniform(splits[1], (SSM_HEAD_TOTAL, SEQUENCE_SPAN), jnp.float32) ** block_scale(splits[1], (SSM_HEAD_TOTAL, SEQUENCE_SPAN), ((0, 4), (1, 8)), -0.2, 0.2)), 0.005, 0.05)
    log_decay = draw_log_decay(jax.random.fold_in(splits[7], 71), 0)
    input_map = bell_draw(splits[3], (SEQUENCE_SPAN, G * N), 0.3, 1.75, ((0, 8), (1, 4)))
    output_map = bell_draw(splits[4], (SEQUENCE_SPAN, G * N), 0.3, 1.75, ((0, 8), (1, 4)))
    skip_gain = jnp.clip(0.5 + 1.5 * jax.random.uniform(splits[5], (SSM_HEAD_TOTAL,), jnp.float32) ** block_scale(splits[5], (SSM_HEAD_TOTAL,), ((0, 4),), -0.2, 0.2), 0.5, 2.0)
    grad_out = draw_grad_out(jax.random.fold_in(splits[7], 71), 0)
    return {"signal": signal, "step_size": step_size, "log_decay": log_decay, "input_map": input_map, "output_map": output_map, "skip_gain": skip_gain, "grad_out": grad_out}


HIGH = lax.Precision.HIGHEST

def block_forward(tokens_in, steps_in, decays_in, keys_in, queries_in, gains_in, block):
    length, groups, heads, width = tokens_in.shape
    entries = keys_in.shape[2]
    number = length // block
    tokens = tokens_in.reshape(number, block, groups, heads, width)
    keys = keys_in.reshape(number, block, groups, entries)
    queries = queries_in.reshape(number, block, groups, entries)
    steps = steps_in.reshape(groups, heads, number, block)
    cumulative = jnp.cumsum(decays_in.reshape(groups, heads, number, block), axis=-1)
    row_ids = lax.broadcasted_iota(jnp.int32, (block, block), 0)
    col_ids = lax.broadcasted_iota(jnp.int32, (block, block), 1)
    lower_mask = row_ids >= col_ids
    spread = cumulative[..., :, None] - cumulative[..., None, :]
    decays = jnp.exp(jnp.where(lower_mask, spread, -jnp.inf))
    scores = jnp.einsum('kqgn,ksgn->gkqs', queries, keys, precision=HIGH)
    weights = decays * scores[:, None] * steps[..., None, :]
    inner = jnp.einsum('ghkqs,ksghp->kqghp', weights, tokens, precision=HIGH)
    tails = jnp.exp(cumulative[..., -1:] - cumulative) * steps
    scaled = tokens * jnp.transpose(tails, (2, 3, 0, 1))[..., None]
    states = jnp.einsum('ksghp,ksgn->kghpn', scaled, keys, precision=HIGH)
    totals = jnp.moveaxis(cumulative[..., -1], -1, 0)

    def advance(carried, item):
        state_now, total_now = item
        return (jnp.exp(total_now)[..., None, None] * carried + state_now, carried)
    zero_state = jnp.zeros((groups, heads, width, entries), jnp.float32)
    final, entering = lax.scan(advance, zero_state, (states, totals))
    outer = jnp.einsum('kqgn,kghpn->kqghp', queries, entering, precision=HIGH)
    outer = outer * jnp.transpose(jnp.exp(cumulative), (2, 3, 0, 1))[..., None]
    result = inner + outer + gains_in[:, :, None] * tokens
    return (result.reshape(length, groups, heads, width), final)

def reference(signal, step_size, log_decay, input_map, output_map, skip_gain, grad_out):
    per_group = SSM_HEAD_TOTAL // G
    sig_all = jnp.transpose(signal.astype(jnp.float32).reshape(SEQUENCE_SPAN, G, per_group, P_SIZE), (1, 0, 2, 3))
    upstream = jnp.transpose(grad_out.astype(jnp.float32).reshape(SEQUENCE_SPAN, G, per_group, P_SIZE), (1, 0, 2, 3))
    steps_all = step_size.reshape(G, per_group, SEQUENCE_SPAN)
    decays_all = log_decay.reshape(G, per_group, SEQUENCE_SPAN)
    keys_all = jnp.transpose(input_map.astype(jnp.float32).reshape(SEQUENCE_SPAN, G, N), (1, 0, 2))
    queries_all = jnp.transpose(output_map.astype(jnp.float32).reshape(SEQUENCE_SPAN, G, N), (1, 0, 2))
    gains_all = skip_gain.reshape(G, per_group)

    def one_group(item):
        sig_one, step_one, decay_one, key_one, query_one, gain_one, upstream_one = item

        def forward_pass(sig_in, step_in, decay_in, key_in, query_in, gain_in):
            return block_forward(sig_in[:, None], step_in[None], decay_in[None], key_in[:, None], query_in[:, None], gain_in[None], BLOCK)
        outputs, pullback = jax.vjp(forward_pass, sig_one, step_one, decay_one, key_one, query_one, gain_one)
        return pullback((upstream_one[:, None], jnp.zeros_like(outputs[1])))
    grads = lax.map(one_group, (sig_all, steps_all, decays_all, keys_all, queries_all, gains_all, upstream))
    grad_signal = jnp.transpose(grads[0], (1, 0, 2, 3)).reshape(SEQUENCE_SPAN, SSM_HEAD_TOTAL * P_SIZE).astype(jnp.bfloat16)
    grad_step = grads[1].reshape(SSM_HEAD_TOTAL, SEQUENCE_SPAN)
    grad_decay = grads[2].reshape(SSM_HEAD_TOTAL, SEQUENCE_SPAN)
    grad_input_map = jnp.transpose(grads[3], (1, 0, 2)).reshape(SEQUENCE_SPAN, G * N).astype(jnp.bfloat16)
    grad_output_map = jnp.transpose(grads[4], (1, 0, 2)).reshape(SEQUENCE_SPAN, G * N).astype(jnp.bfloat16)
    grad_skip = grads[5].reshape(SSM_HEAD_TOTAL)
    return (grad_signal, grad_step, grad_decay, grad_input_map, grad_output_map, grad_skip)
```

```python
import functools

import jax
import jax.numpy as jnp
from jax import lax
from jax.experimental import pallas as pl
from jax.experimental.pallas import tpu as pltpu
from jax.sharding import PartitionSpec as P

P_SIZE = 64
N = 128
C = 128
LOG2E = 1.4426950408889634
F32 = jnp.float32
BF16 = jnp.bfloat16
NT = (((1,), (1,)), ((), ()))
TN = (((0,), (0,)), ((), ()))
NN = (((1,), (0,)), ((), ()))


def dot(a, b, dims):
    return lax.dot_general(a, b, dims, preferred_element_type=F32)


def split(a):
    high = a.astype(BF16)
    return high, (a - high.astype(F32)).astype(BF16)


def halves():
    lane = lax.broadcasted_iota(jnp.int32, (1, 2 * P_SIZE), 1)
    low = (lane < P_SIZE).astype(F32)
    return low, 1.0 - low


def blocks_of(pair):
    low, high = halves()
    return jnp.concatenate([pair * low.astype(pair.dtype), pair * high.astype(pair.dtype)], axis=0)


def params(**more):
    return pltpu.CompilerParams(vmem_limit_bytes=48 * 1024 * 1024, **more)


def prep_kernel(groups, per, decay_ref, step_ref, col_ref, row_ref):
    heads = decay_ref.shape[0]
    lane = lax.broadcasted_iota(jnp.int32, (heads, C), 1)
    for k in range(decay_ref.shape[1] // C):
        at = slice(k * C, (k + 1) * C)
        step = step_ref[:, at]
        cum = decay_ref[:, at]
        shift = 1
        while shift < C:
            cum = cum + jnp.where(lane >= shift, pltpu.roll(cum, shift, 1), 0.0)
            shift *= 2
        total = cum[:, C - 1 :]
        cum2 = cum * LOG2E
        row_ref[:, at] = cum2 - jnp.log(step) * LOG2E
        rise = jnp.exp(cum)
        tail = jnp.exp(total - cum) * step
        for g in range(groups):
            own = slice(g * per, (g + 1) * per)
            pad = jnp.zeros((C - 3 * per, C), F32)
            stacked = jnp.concatenate([cum2[own], rise[own], tail[own], pad], axis=0)
            col_ref[at, g * C : (g + 1) * C] = stacked.T


def state_kernel(per, x_ref, dy_ref, k_ref, q_ref, colx_ref, coly_ref, ex_ref, ey_ref,
                 h_ref, g_ref, ends_ref, h_s, g_s):
    k = pl.program_id(1)

    @pl.when(k == 0)
    def _():
        h_s[...] = jnp.zeros_like(h_s)
        g_s[...] = jnp.zeros_like(g_s)

    low, _ = halves()
    keys = jnp.concatenate([k_ref[...]] * 2, axis=0)
    queries = jnp.concatenate([q_ref[...]] * 2, axis=0)
    colx = colx_ref[...]
    coly = coly_ref[...]

    def scaled(ref, col, first):
        parts = []
        for j in range(per // 2):
            a = first + 2 * j
            factor = jnp.where(low > 0, col[:, a : a + 1], col[:, a + 1 : a + 2])
            parts.append(ref[:, 128 * j : 128 * (j + 1)].astype(F32) * factor)
        return jnp.concatenate(split(jnp.concatenate(parts, axis=1)), axis=0)

    h_ref[0] = h_s[...]
    g_ref[0] = g_s[...]
    h_s[...] = ex_ref[0] * h_s[...] + dot(keys, scaled(x_ref, colx, 2 * per), TN)
    g_s[...] = ey_ref[0] * g_s[...] + dot(queries, scaled(dy_ref, coly, per), TN)

    @pl.when(k == pl.num_programs(1) - 1)
    def _():
        ends_ref[0] = h_s[...]
        ends_ref[1] = g_s[...]


def inner_kernel(per, carried, x_ref, dy_ref, k_ref, q_ref, col_ref, row_ref, *rest):
    z_ref, gq_ref, gk_ref, r_ref, skip_ref = rest[carried:]
    lane = lax.broadcasted_iota(jnp.int32, (C, C), 1)
    mask = lax.broadcasted_iota(jnp.int32, (C, C), 0) >= lane
    keys = k_ref[...]
    queries = q_ref[...]
    scores = dot(queries, keys, NT)
    col = col_ref[...]
    row = row_ref[...]
    total = jnp.zeros((C, C), F32)
    sums = jnp.zeros((C, C), F32)
    for j in range(per // 2):
        at = slice(128 * j, 128 * (j + 1))
        x = x_ref[:, at]
        dy = dy_ref[:, at]
        met = dot(dy, blocks_of(x), NT)
        highs, lows = [], []
        for i in range(2):
            a = 2 * j + i
            spread = jnp.where(mask, col[:, a : a + 1] - row[a : a + 1, :], -1e4)
            decay = jnp.exp2(spread)
            lm = decay * met[:, i * C : (i + 1) * C]
            total = total + lm
            sums = jnp.where(lane == a, jnp.sum(lm * scores, axis=1, keepdims=True), sums)
            high, rest_of = split(decay * scores)
            highs.append(high)
            lows.append(rest_of)
        ups = blocks_of(dy)
        z_ref[:, at] = dot(jnp.concatenate(highs, axis=0), ups, TN) + dot(
            jnp.concatenate(lows, axis=0), ups, TN
        )
        skip_ref[0, :, at] = jnp.sum(x.astype(F32) * dy.astype(F32), axis=0, keepdims=True)
    high, rest_of = split(total)
    gq_ref[...] = dot(high, keys, NN) + dot(rest_of, keys, NN)
    gk_ref[...] = dot(high, queries, TN) + dot(rest_of, queries, TN)
    r_ref[...] = sums


def outer_kernel(per, x_ref, dy_ref, k_ref, q_ref, col_ref, step_ref, h_ref, g_ref, ends_ref,
                 pre_ref, post_ref, tot_ref, gain_ref, z_ref, gq_ref, gk_ref, r_ref,
                 gx_ref, gstep_ref, gdecay_ref, gkey_ref, gquery_ref):
    lane = lax.broadcasted_iota(jnp.int32, (C, C), 1)
    last = lax.broadcasted_iota(jnp.int32, (C, C), 0) == C - 1
    low, high_half = halves()
    keys2 = jnp.concatenate([k_ref[...]] * 2, axis=1)
    queries = q_ref[...].astype(F32)
    col = col_ref[...]
    gq = gq_ref[...]
    gk = gk_ref[...]
    pack = r_ref[...]
    for j in range(per // 2):
        at = slice(128 * j, 128 * (j + 1))
        x = x_ref[:, at]
        dy = dy_ref[:, at]
        state = h_ref[0, :, at] + pre_ref[0, :, at] * ends_ref[0, :, at]
        pull = g_ref[0, :, at] + post_ref[0, :, at] * ends_ref[1, :, at]
        s_high, s_low = split(state)
        p_high, p_low = split(pull)
        s_both = jnp.concatenate([blocks_of(s_high), blocks_of(s_low)], axis=1)
        p_both = jnp.concatenate([blocks_of(p_high), blocks_of(p_low)], axis=1)
        to_q = dot(jnp.concatenate([dy, dy], axis=1), s_both, NT)
        to_k = dot(jnp.concatenate([x, x], axis=1), p_both, NT)
        z_out = dot(keys2, jnp.concatenate([p_high, p_low], axis=0), NN)
        a = 2 * j
        tails = [col[:, 2 * per + a + i : 2 * per + a + i + 1] for i in range(2)]
        z_out = z_out * jnp.where(low > 0, tails[0], tails[1])
        z = z_ref[:, at] + z_out
        gx_ref[:, at] = (z + gain_ref[:, at] * dy.astype(F32)).astype(BF16)
        xf = x.astype(F32)
        xz = xf * z
        edge = jnp.sum(xf * z_out + tot_ref[0, :, at] * (state * pull), axis=0, keepdims=True)
        for i, half in enumerate((low, high_half)):
            rise = col[:, per + a + i : per + a + i + 1]
            own = to_q[:, i * C : (i + 1) * C] * rise
            gq = gq + own
            gk = gk + to_k[:, i * C : (i + 1) * C] * tails[i]
            rows = jnp.sum(own * queries, axis=1, keepdims=True)
            cols = jnp.sum(xz * half, axis=1, keepdims=True)
            edge_sum = jnp.sum(edge * half, axis=1, keepdims=True)
            pack = jnp.where(lane == a + i, pack + (rows - cols), pack)
            pack = jnp.where((lane == a + i) & last, pack + edge_sum, pack)
            pack = jnp.where(lane == per + a + i, cols, pack)
    gquery_ref[...] = gq.astype(BF16)
    gkey_ref[...] = gk.astype(BF16)
    turned = pack.T
    part = turned[:per]
    lane16 = lax.broadcasted_iota(jnp.int32, (per, C), 1)
    shift = 1
    while shift < C:
        part = part + jnp.where(lane16 < C - shift, pltpu.roll(part, C - shift, 1), 0.0)
        shift *= 2
    gdecay_ref[...] = part
    gstep_ref[...] = turned[per : 2 * per] / step_ref[...]


def exchange(parts, nx, x, nz):
    kept = lax.dynamic_index_in_dim(parts, x, 1, False)
    got = [kept]
    for r in range(1, nx):
        pairs = [(c * nx + i, c * nx + (i + r) % nx) for c in range(nz) for i in range(nx)]
        sent = lax.dynamic_index_in_dim(parts, (x + r) % nx, 1, False)
        got.append(lax.ppermute(sent, "ctx", pairs))
    return got


def by_sender(got, nx, x):
    out = []
    for j in range(nx):
        one = got[0]
        for r in range(1, nx):
            one = jnp.where((x - j) % nx == r, got[r], one)
        out.append(one)
    return out


def held(value, work):
    return lax.optimization_barrier((value, work))


def carry(ends, fade, stages, work):
    count = lax.axis_size("ctx")
    nx = 2 if count < 16 else 4
    nz = count // nx
    place = lax.axis_index("ctx")
    x, z = place % nx, place // nx
    turns = [[(c * nx + i, c * nx + (i + r) % nx) for c in range(nz) for i in range(nx)] for r in range(nx)]
    row_fade = by_sender([fade] + [lax.ppermute(fade, "ctx", t) for t in turns[1:]], nx, x)
    all_fade = functools.reduce(lambda a, b: a * b, row_fade)

    _, rows, width = ends.shape
    got = exchange(ends.reshape(2, nx, rows // nx, width), nx, x, nz)
    work = stages[0](work)
    got, work = held(got, work)
    both = by_sender(got, nx, x)
    states, pulls = [b[0] for b in both], [b[1] for b in both]
    state_sum = states[0]
    for i in range(1, nx):
        state_sum = row_fade[i] * state_sum + states[i]
    pull_sum = pulls[nx - 1]
    for i in range(nx - 2, -1, -1):
        pull_sum = row_fade[i] * pull_sum + pulls[i]
    entering, leaving, up_send, down_send = None, None, state_sum, pull_sum
    for hop in range(nz - 1):
        up = [(hop * nx + i, (hop + 1) * nx + i) for i in range(nx)]
        down = [((nz - 1 - hop) * nx + i, (nz - 2 - hop) * nx + i) for i in range(nx)]
        came = (lax.ppermute(up_send, "ctx", up), lax.ppermute(down_send, "ctx", down))
        work = stages[1 + hop](work)
        came, work = held(came, work)
        entering = came[0] if hop == 0 else entering + came[0]
        leaving = came[1] if hop == 0 else leaving + came[1]
        up_send = all_fade * entering + state_sum
        down_send = all_fade * leaving + pull_sum
    ins, outs = [entering], [leaving]
    for i in range(nx - 1):
        ins.append(row_fade[i] * ins[-1] + states[i])
    for i in range(nx - 1, 0, -1):
        outs.append(row_fade[i] * outs[-1] + pulls[i])
    got = exchange(jnp.stack([jnp.stack(ins), jnp.stack(outs[::-1])]), nx, x, nz)
    work = stages[nz](work)
    got, work = held(got, work)
    both = jnp.stack(by_sender(got, nx, x), axis=1)
    return both.reshape(2, rows, width), work


def on_device(signal, step_size, log_decay, input_map, output_map, skip_gain, grad_out):
    heads, length = step_size.shape
    groups = input_map.shape[1] // N
    per = heads // groups
    wide = per * P_SIZE
    width = heads * P_SIZE
    nk = length // C

    col, row = pl.pallas_call(
        functools.partial(prep_kernel, groups, per),
        out_shape=(
            jax.ShapeDtypeStruct((length, groups * C), F32),
            jax.ShapeDtypeStruct((heads, length), F32),
        ),
        compiler_params=params(),
        name="prep",
    )(log_decay, step_size)

    sums = jnp.sum(log_decay.reshape(heads, nk, C), axis=-1)
    after = lax.broadcasted_iota(jnp.int32, (nk, nk), 0) > lax.broadcasted_iota(jnp.int32, (nk, nk), 1)
    before = jnp.sum(jnp.where(after.T[None], sums[:, :, None], 0.0), axis=1)
    behind = jnp.sum(jnp.where(after[None], sums[:, :, None], 0.0), axis=1)

    def lanes(a):
        return jnp.repeat(jnp.exp(a.T), P_SIZE, axis=1)[:, None, :]

    tot, pre, post = lanes(sums), lanes(before), lanes(behind)
    gains = jnp.repeat(skip_gain, P_SIZE)[None, :]

    def spec(shape, index):
        return pl.BlockSpec(shape, index)

    big = spec((C, wide), lambda g, k: (k, g))
    big_r = spec((C, wide), lambda g, k: (nk - 1 - k, g))
    small = spec((C, C), lambda g, k: (k, g))
    small_r = spec((C, C), lambda g, k: (nk - 1 - k, g))
    line = spec((1, 1, wide), lambda g, k: (k, 0, g))
    line_r = spec((1, 1, wide), lambda g, k: (nk - 1 - k, 0, g))
    local = spec((1, N, wide), lambda g, k: (k, 0, g))
    local_r = spec((1, N, wide), lambda g, k: (nk - 1 - k, 0, g))
    end = spec((2, N, wide), lambda g, k: (0, 0, g))
    rowed = spec((per, C), lambda g, k: (g, k))

    states, pulls, ends = pl.pallas_call(
        functools.partial(state_kernel, per),
        grid=(groups, nk),
        in_specs=[big, big_r, small, small_r, small, small_r, line, line_r],
        out_specs=(local, local_r, end),
        out_shape=(
            jax.ShapeDtypeStruct((nk, N, width), F32),
            jax.ShapeDtypeStruct((nk, N, width), F32),
            jax.ShapeDtypeStruct((2, N, width), F32),
        ),
        scratch_shapes=[pltpu.VMEM((N, wide), F32), pltpu.VMEM((N, wide), F32)],
        compiler_params=params(),
        cost_estimate=pl.CostEstimate(flops=8 * length * width * N, bytes_accessed=24 << 20, transcendentals=0),
        name="states",
    )(signal, grad_out, input_map, output_map, col, col, tot, tot)

    inner_shapes = (
        jax.ShapeDtypeStruct((length, width), F32),
        jax.ShapeDtypeStruct((length, groups * N), F32),
        jax.ShapeDtypeStruct((length, groups * N), F32),
        jax.ShapeDtypeStruct((length, groups * C), F32),
        jax.ShapeDtypeStruct((nk, 1, width), F32),
    )
    def inner(first, each, carried):
        def moved(shape, kind):
            if kind == "tok":
                return spec(shape, lambda g, k: (first + k, g))
            if kind == "row":
                return spec(shape, lambda g, k: (g, first + k))
            return spec(shape, lambda g, k: (first + k, 0, g))

        b, s = moved((C, wide), "tok"), moved((C, C), "tok")
        return pl.pallas_call(
            functools.partial(inner_kernel, per, len(carried)),
            grid=(groups, each),
            in_specs=[b, b, s, s, s, moved((per, C), "row")]
            + [pl.BlockSpec(memory_space=pl.ANY)] * len(carried),
            out_specs=(b, s, s, s, moved((1, 1, wide), "line")),
            out_shape=inner_shapes,
            input_output_aliases={6 + i: i for i in range(len(carried))},
            compiler_params=params(),
            cost_estimate=pl.CostEstimate(
                flops=8_000_000_000 * each // nk * 4, bytes_accessed=(16 << 20) * each // nk, transcendentals=0
            ),
            name="inner",
        )(signal, grad_out, input_map, output_map, col, row, *carried)

    count = lax.axis_size("ctx")
    hops = count // (2 if count < 16 else 4) + 1
    marks = [round(i * nk / hops) for i in range(hops + 1)]

    def stage(i):
        def run(carried):
            first, each = marks[i], marks[i + 1] - marks[i]
            return inner(first, each, carried) if each else carried

        return run

    fade = jnp.repeat(jnp.exp(jnp.sum(sums, axis=1)), P_SIZE)[None, :]
    carried_ends, carried = carry(ends, fade, [stage(i) for i in range(hops)], ())
    z, gq, gk, r, skip = carried

    grad_skip = lax.psum(jnp.sum(skip.reshape(nk, heads, P_SIZE), axis=(0, 2)), "ctx")

    grad_signal, grad_step, grad_decay, grad_input, grad_output = pl.pallas_call(
        functools.partial(outer_kernel, per),
        grid=(groups, nk),
        in_specs=[big, big, small, small, small, rowed, local, local, end, line, line, line,
                  spec((1, wide), lambda g, k: (0, g)), big, small, small, small],
        out_specs=(big, rowed, rowed, small, small),
        out_shape=(
            jax.ShapeDtypeStruct((length, width), BF16),
            jax.ShapeDtypeStruct((heads, length), F32),
            jax.ShapeDtypeStruct((heads, length), F32),
            jax.ShapeDtypeStruct((length, groups * N), BF16),
            jax.ShapeDtypeStruct((length, groups * N), BF16),
        ),
        compiler_params=params(),
        cost_estimate=pl.CostEstimate(flops=16 * length * width * N, bytes_accessed=40 << 20, transcendentals=0),
        name="outer",
    )(signal, grad_out, input_map, output_map, col, step_size, states, pulls, carried_ends,
      pre, post, tot, gains, z, gq, gk, r)
    return (grad_signal, grad_step, grad_decay, grad_input, grad_output, grad_skip)


def solution(mesh):
    placed = (
        P("ctx", "head"),
        P("head", "ctx"),
        P("head", "ctx"),
        P("ctx", "head"),
        P("ctx", "head"),
        P("head"),
        P("ctx", "head"),
    )
    return jax.shard_map(
        on_device,
        mesh=mesh,
        in_specs=placed,
        out_specs=(
            P("ctx", "head"),
            P("head", "ctx"),
            P("head", "ctx"),
            P("ctx", "head"),
            P("ctx", "head"),
            P("head"),
        ),
        check_vma=False,
    )
```

```python
import functools

import jax
import jax.numpy as jnp
from jax import lax
from jax.experimental import pallas as pl
from jax.experimental.pallas import tpu as pltpu
from jax.sharding import PartitionSpec as P

P_SIZE = 64
N = 128
C = 128
LOG2E = 1.4426950408889634
F32 = jnp.float32
BF16 = jnp.bfloat16
NT = (((1,), (1,)), ((), ()))
TN = (((0,), (0,)), ((), ()))
NN = (((1,), (0,)), ((), ()))


def dot(a, b, dims):
    return lax.dot_general(a, b, dims, preferred_element_type=F32)


def split(a):
    high = a.astype(BF16)
    return high, (a - high.astype(F32)).astype(BF16)


def halves():
    lane = lax.broadcasted_iota(jnp.int32, (1, 2 * P_SIZE), 1)
    low = (lane < P_SIZE).astype(F32)
    return low, 1.0 - low


def blocks_of(pair):
    low, high = halves()
    return jnp.concatenate([pair * low.astype(pair.dtype), pair * high.astype(pair.dtype)], axis=0)


def params(**more):
    return pltpu.CompilerParams(vmem_limit_bytes=48 * 1024 * 1024, **more)


def prep_kernel(groups, per, decay_ref, step_ref, col_ref, row_ref):
    heads = decay_ref.shape[0]
    lane = lax.broadcasted_iota(jnp.int32, (heads, C), 1)
    for k in range(decay_ref.shape[1] // C):
        at = slice(k * C, (k + 1) * C)
        step = step_ref[:, at]
        cum = decay_ref[:, at]
        shift = 1
        while shift < C:
            cum = cum + jnp.where(lane >= shift, pltpu.roll(cum, shift, 1), 0.0)
            shift *= 2
        total = cum[:, C - 1 :]
        cum2 = cum * LOG2E
        low2 = cum2 - jnp.log(step) * LOG2E
        rise = jnp.exp(cum)
        tail = jnp.exp(total - cum) * step
        for g in range(groups):
            own = slice(g * per, (g + 1) * per)
            pad = jnp.zeros((C - 3 * per, C), F32)
            stacked = jnp.concatenate([low2[own], rise[own], tail[own], pad], axis=0)
            rows = jnp.concatenate([cum2[own], rise[own], tail[own]], axis=0)
            row_ref[g * 3 * per : (g + 1) * 3 * per, at] = rows
            col_ref[at, g * C : (g + 1) * C] = stacked.T


def state_kernel(per, x_ref, dy_ref, k_ref, q_ref, col_ref, tot_ref, pre_ref,
                 h_ref, u_ref, ends_ref, skip_ref, h_s, g_s):
    k = pl.program_id(1)

    @pl.when(k == 0)
    def _():
        h_s[...] = jnp.zeros_like(h_s)
        g_s[...] = jnp.zeros_like(g_s)
        skip_ref[...] = jnp.zeros_like(skip_ref)

    low, _ = halves()
    keys = jnp.concatenate([k_ref[...]] * 2, axis=0)
    queries = jnp.concatenate([q_ref[...]] * 2, axis=0)
    col = col_ref[...]

    def scaled(ref, first):
        parts = []
        for j in range(per // 2):
            a = first + 2 * j
            factor = jnp.where(low > 0, col[:, a : a + 1], col[:, a + 1 : a + 2])
            parts.append(ref[:, 128 * j : 128 * (j + 1)].astype(F32) * factor)
        return jnp.concatenate(split(jnp.concatenate(parts, axis=1)), axis=0)

    h_ref[0] = h_s[...]
    h_s[...] = tot_ref[0] * h_s[...] + dot(keys, scaled(x_ref, 2 * per), TN)
    pull = dot(queries, scaled(dy_ref, per), TN)
    u_ref[0] = pull
    g_s[...] = g_s[...] + pre_ref[0] * pull
    both = x_ref[...].astype(F32) * dy_ref[...].astype(F32)
    skip_ref[...] = skip_ref[...] + jnp.sum(both, axis=0, keepdims=True)

    @pl.when(k == pl.num_programs(1) - 1)
    def _():
        ends_ref[0] = h_s[...]
        ends_ref[1] = g_s[...]


def inner_kernel(per, carried, x_ref, dy_ref, k_ref, q_ref, col_ref, row_ref, *rest):
    z_ref, gq_ref, gk_ref, rc_ref, c_s = rest[carried:]
    mask = lax.broadcasted_iota(jnp.int32, (C, C), 1) >= lax.broadcasted_iota(jnp.int32, (C, C), 0)
    keys = k_ref[...]
    queries = q_ref[...]
    scores = dot(keys, queries, NT)
    total = jnp.zeros((C, C), F32)
    for j in range(per // 2):
        at = slice(128 * j, 128 * (j + 1))
        ups = blocks_of(dy_ref[:, at])
        met = dot(x_ref[:, at], ups, NT)
        highs, lows = [], []
        for i in range(2):
            a = 2 * j + i
            spread = jnp.where(mask, row_ref[a : a + 1, :] - col_ref[:, a : a + 1], -1e4)
            decay = jnp.exp2(spread)
            lm = decay * met[:, i * C : (i + 1) * C]
            total = total + lm
            both = lm * scores
            rc_ref[a : a + 1, :] = jnp.sum(both, axis=0, keepdims=True)
            c_s[:, a : a + 1] = jnp.sum(both, axis=1, keepdims=True)
            high, rest_of = split(decay * scores)
            highs.append(high)
            lows.append(rest_of)
        z_ref[:, at] = dot(jnp.concatenate(highs, axis=1), ups, NN) + dot(
            jnp.concatenate(lows, axis=1), ups, NN
        )
    high, rest_of = split(total)
    gq_ref[...] = dot(high, keys, TN) + dot(rest_of, keys, TN)
    gk_ref[...] = dot(high, queries, NN) + dot(rest_of, queries, NN)
    rc_ref[per:, :] = c_s[...].T[:per]


def outer_kernel(per, nx, x_ref, dy_ref, k_ref, q_ref, col_ref, row_ref, step_ref, h_ref, u_ref,
                 tot_ref, pre_ref, gain_ref, z_ref, gq_ref, gk_ref, rc_ref, *rest):
    got = rest[:nx]
    gx_ref, gstep_ref, gdecay_ref, gkey_ref, gquery_ref, e_s, g_s, r_s, c_s, edge_s = rest[nx:]
    place = lax.rem(lax.axis_index("ctx"), nx)

    @pl.when(pl.program_id(1) == 0)
    def _():
        size = N // nx
        for r in range(nx):
            part = pl.ds(pl.multiple_of(lax.rem(place - r + nx, nx) * size, size), size)
            e_s[part, :] = got[r][0]
            g_s[part, :] = got[r][1]

    low, high_half = halves()
    keys2 = jnp.concatenate([k_ref[...]] * 2, axis=1)
    keys_t = k_ref[...].astype(F32).T
    queries_t = q_ref[...].astype(F32).T
    gq = jnp.zeros((N, C), F32)
    gk = jnp.zeros((N, C), F32)
    for j in range(per // 2):
        at = slice(128 * j, 128 * (j + 1))
        x = x_ref[:, at]
        dy = dy_ref[:, at]
        pull = g_s[:, at]
        tot = tot_ref[0, :, at]
        state = h_ref[0, :, at] + pre_ref[0, :, at] * e_s[:, at]
        g_s[:, at] = tot * pull + u_ref[0, :, at]
        edge = jnp.sum(state * pull, axis=0, keepdims=True) * tot
        s_high, s_low = split(state)
        p_high, p_low = split(pull)
        s_both = jnp.concatenate([blocks_of(s_high), blocks_of(s_low)], axis=1)
        p_both = jnp.concatenate([blocks_of(p_high), blocks_of(p_low)], axis=1)
        to_q = dot(s_both, jnp.concatenate([dy, dy], axis=1), NT)
        to_k = dot(p_both, jnp.concatenate([x, x], axis=1), NT)
        z_out = dot(keys2, jnp.concatenate([p_high, p_low], axis=0), NN)
        a = 2 * j
        tails = [col_ref[:, 2 * per + a + i : 2 * per + a + i + 1] for i in range(2)]
        z = z_ref[:, at] + z_out * jnp.where(low > 0, tails[0], tails[1])
        gx_ref[:, at] = (z + gain_ref[0, :, at] * dy.astype(F32)).astype(BF16)
        for i, half in enumerate((low, high_half)):
            own_q = to_q[i * N : (i + 1) * N] * row_ref[per + a + i : per + a + i + 1, :]
            own_k = to_k[i * N : (i + 1) * N] * row_ref[2 * per + a + i : 2 * per + a + i + 1, :]
            gq = gq + own_q
            gk = gk + own_k
            r_s[a + i : a + i + 1, :] = jnp.sum(own_q * queries_t, axis=0, keepdims=True)
            c_s[a + i : a + i + 1, :] = jnp.sum(own_k * keys_t, axis=0, keepdims=True)
            edge_s[a + i : a + i + 1, :] = edge * half
    gquery_ref[...] = (gq_ref[...] + gq.T).astype(BF16)
    gkey_ref[...] = (gk_ref[...] + gk.T).astype(BF16)
    cols = rc_ref[per:, :] + c_s[...]
    part = rc_ref[:per, :] + r_s[...] - cols
    edge_sum = jnp.sum(edge_s[...] + c_s[...], axis=1, keepdims=True)
    lane = lax.broadcasted_iota(jnp.int32, (per, C), 1)
    part = jnp.where(lane == C - 1, part + edge_sum, part)
    shift = 1
    while shift < C:
        part = part + jnp.where(lane < C - shift, pltpu.roll(part, C - shift, 1), 0.0)
        shift *= 2
    gdecay_ref[...] = part
    gstep_ref[...] = cols / step_ref[...]


def exchange(parts, nx, x, nz):
    kept = lax.dynamic_index_in_dim(parts, x, 1, False)
    got = [kept]
    for r in range(1, nx):
        pairs = [(c * nx + i, c * nx + (i + r) % nx) for c in range(nz) for i in range(nx)]
        sent = lax.dynamic_index_in_dim(parts, (x + r) % nx, 1, False)
        got.append(lax.ppermute(sent, "ctx", pairs))
    return got


def by_sender(got, nx, x):
    out = []
    for j in range(nx):
        one = got[0]
        for r in range(1, nx):
            one = jnp.where((x - j) % nx == r, got[r], one)
        out.append(one)
    return out


def held(value, work):
    return lax.optimization_barrier((value, work))


def carry(ends, fade, skip, stages, work):
    count = lax.axis_size("ctx")
    nx = 2 if count < 16 else 4
    nz = count // nx
    place = lax.axis_index("ctx")
    x, z = place % nx, place // nx
    turns = [[(c * nx + i, c * nx + (i + r) % nx) for c in range(nz) for i in range(nx)] for r in range(nx)]
    line = jnp.concatenate([fade, skip], axis=0)
    lines = [line] + [lax.ppermute(line, "ctx", t) for t in turns[1:]]
    _, rows, width = ends.shape
    got = exchange(ends.reshape(2, nx, rows // nx, width), nx, x, nz)
    work = stages[0](work)
    (got, lines), work = held((got, lines), work)
    lines = by_sender(lines, nx, x)
    row_fade = [one[:1] for one in lines]
    all_fade = functools.reduce(lambda a, b: a * b, row_fade)
    skip = functools.reduce(lambda a, b: a + b, [one[1:] for one in lines])
    skips = [skip]
    for r in range(1, nz):
        skips.append(lax.ppermute(skip, "ctx", [(c * nx + i, (c + r) % nz * nx + i) for c in range(nz) for i in range(nx)]))
    both = by_sender(got, nx, x)
    states, pulls = [b[0] for b in both], [b[1] for b in both]
    state_sum = states[0]
    for i in range(1, nx):
        state_sum = row_fade[i] * state_sum + states[i]
    pull_sum = pulls[nx - 1]
    for i in range(nx - 2, -1, -1):
        pull_sum = row_fade[i] * pull_sum + pulls[i]
    entering, leaving, up_send, down_send = None, None, state_sum, pull_sum
    for hop in range(nz - 1):
        up = [(hop * nx + i, (hop + 1) * nx + i) for i in range(nx)]
        down = [((nz - 1 - hop) * nx + i, (nz - 2 - hop) * nx + i) for i in range(nx)]
        came = (lax.ppermute(up_send, "ctx", up), lax.ppermute(down_send, "ctx", down))
        work = stages[1 + hop](work)
        if hop == 0:
            (came, skips), work = held((came, skips), work)
            skip = functools.reduce(lambda a, b: a + b, by_sender(skips, nz, z))
        else:
            came, work = held(came, work)
        entering = came[0] if hop == 0 else entering + came[0]
        leaving = came[1] if hop == 0 else leaving + came[1]
        up_send = all_fade * entering + state_sum
        down_send = all_fade * leaving + pull_sum
    ins, outs = [entering], [leaving]
    for i in range(nx - 1):
        ins.append(row_fade[i] * ins[-1] + states[i])
    for i in range(nx - 1, 0, -1):
        outs.append(row_fade[i] * outs[-1] + pulls[i])
    got = exchange(jnp.stack([jnp.stack(ins), jnp.stack(outs[::-1])]), nx, x, nz)
    work = stages[nz](work)
    got, work = held(got, work)
    return got, skip, work


def on_device(signal, step_size, log_decay, input_map, output_map, skip_gain, grad_out):
    heads, length = step_size.shape
    groups = input_map.shape[1] // N
    per = heads // groups
    wide = per * P_SIZE
    width = heads * P_SIZE
    nk = length // C

    col, row = pl.pallas_call(
        functools.partial(prep_kernel, groups, per),
        out_shape=(
            jax.ShapeDtypeStruct((length, groups * C), F32),
            jax.ShapeDtypeStruct((3 * heads, length), F32),
        ),
        compiler_params=params(),
        name="prep",
    )(log_decay, step_size)

    sums = jnp.sum(log_decay.reshape(heads, nk, C), axis=-1)
    after = lax.broadcasted_iota(jnp.int32, (nk, nk), 0) < lax.broadcasted_iota(jnp.int32, (nk, nk), 1)
    before = jnp.sum(jnp.where(after[None], sums[:, :, None], 0.0), axis=1)
    span = jnp.sum(sums, axis=1)
    chunk_lines = jnp.exp(jnp.concatenate([sums.T, before.T, span[None]], axis=0))
    lines = jnp.concatenate([chunk_lines, skip_gain[None]], axis=0)
    lines = jnp.repeat(lines, P_SIZE, axis=1)[:, None, :]
    fade = lines[2 * nk]

    def spec(shape, index):
        return pl.BlockSpec(shape, index)

    def specs(at):
        return (
            spec((C, wide), lambda g, k: (at(k), g)),
            spec((C, C), lambda g, k: (at(k), g)),
            spec((1, N, wide), lambda g, k: (at(k), 0, g)),
            spec((1, 1, wide), lambda g, k: (at(k), 0, g)),
            spec((1, 1, wide), lambda g, k: (nk + at(k), 0, g)),
        )

    big, small, local, tot, pre = specs(lambda k: k)

    states, pulls, ends, skip = pl.pallas_call(
        functools.partial(state_kernel, per),
        grid=(groups, nk),
        in_specs=[big, big, small, small, small, tot, pre],
        out_specs=(local, local, spec((2, N, wide), lambda g, k: (0, 0, g)), spec((1, wide), lambda g, k: (0, g))),
        out_shape=(
            jax.ShapeDtypeStruct((nk, N, width), F32),
            jax.ShapeDtypeStruct((nk, N, width), F32),
            jax.ShapeDtypeStruct((2, N, width), F32),
            jax.ShapeDtypeStruct((1, width), F32),
        ),
        scratch_shapes=[pltpu.VMEM((N, wide), F32), pltpu.VMEM((N, wide), F32)],
        compiler_params=params(),
        cost_estimate=pl.CostEstimate(flops=8 * length * width * N, bytes_accessed=24 << 20, transcendentals=0),
        name="states",
    )(signal, grad_out, input_map, output_map, col, lines, lines)

    inner_shapes = (
        jax.ShapeDtypeStruct((length, width), F32),
        jax.ShapeDtypeStruct((length, groups * N), F32),
        jax.ShapeDtypeStruct((length, groups * N), F32),
        jax.ShapeDtypeStruct((2 * heads, length), F32),
    )
    def inner(first, each, carried):
        b, s, _, _, _ = specs(lambda k: first + k)
        return pl.pallas_call(
            functools.partial(inner_kernel, per, len(carried)),
            grid=(groups, each),
            in_specs=[b, b, s, s, s, spec((3 * per, C), lambda g, k: (g, first + k))]
            + [pl.BlockSpec(memory_space=pltpu.HBM)] * len(carried),
            out_specs=(b, s, s, spec((2 * per, C), lambda g, k: (g, first + k))),
            out_shape=inner_shapes,
            scratch_shapes=[pltpu.VMEM((C, C), F32)],
            input_output_aliases={6 + i: i for i in range(len(carried))},
            compiler_params=params(),
            cost_estimate=pl.CostEstimate(
                flops=8_000_000_000 * each // nk * 4, bytes_accessed=(16 << 20) * each // nk, transcendentals=0
            ),
            name="inner",
        )(signal, grad_out, input_map, output_map, col, row, *carried)

    count = lax.axis_size("ctx")
    hops = count // (2 if count < 16 else 4) + 1
    marks = [round(i * nk / hops) for i in range(hops + 1)]

    def stage(i):
        def run(carried):
            first, each = marks[i], marks[i + 1] - marks[i]
            return inner(first, each, carried) if each else carried

        return run

    got, skip, carried = carry(ends, fade, skip, [stage(i) for i in range(hops)], ())
    z, gq, gk, rc = carried
    nx = len(got)
    grad_skip = jnp.sum(skip.reshape(heads, P_SIZE), axis=1)

    def back(k):
        return nk - 1 - k

    big, small, local, tot, pre = specs(back)
    rowed = spec((per, C), lambda g, k: (g, back(k)))
    grad_signal, grad_step, grad_decay, grad_input, grad_output = pl.pallas_call(
        functools.partial(outer_kernel, per, nx),
        grid=(groups, nk),
        in_specs=[big, big, small, small, small, spec((3 * per, C), lambda g, k: (g, back(k))), rowed,
                  local, local, tot, pre, spec((1, 1, wide), lambda g, k: (2 * nk + 1, 0, g)),
                  big, small, small, spec((2 * per, C), lambda g, k: (g, back(k)))]
        + [spec((2, N // nx, wide), lambda g, k: (0, 0, g))] * nx,
        out_specs=(big, rowed, rowed, small, small),
        out_shape=(
            jax.ShapeDtypeStruct((length, width), BF16),
            jax.ShapeDtypeStruct((heads, length), F32),
            jax.ShapeDtypeStruct((heads, length), F32),
            jax.ShapeDtypeStruct((length, groups * N), BF16),
            jax.ShapeDtypeStruct((length, groups * N), BF16),
        ),
        scratch_shapes=[
            pltpu.VMEM((N, wide), F32),
            pltpu.VMEM((N, wide), F32),
            pltpu.VMEM((per, C), F32),
            pltpu.VMEM((per, C), F32),
            pltpu.VMEM((per, C), F32),
        ],
        compiler_params=params(),
        cost_estimate=pl.CostEstimate(flops=16 * length * width * N, bytes_accessed=40 << 20, transcendentals=0),
        name="outer",
    )(signal, grad_out, input_map, output_map, col, row, step_size, states, pulls,
      lines, lines, lines, z, gq, gk, rc, *got)
    return (grad_signal, grad_step, grad_decay, grad_input, grad_output, grad_skip)


def solution(mesh):
    placed = (
        P("ctx", "head"),
        P("head", "ctx"),
        P("head", "ctx"),
        P("ctx", "head"),
        P("ctx", "head"),
        P("head"),
        P("ctx", "head"),
    )
    return jax.shard_map(
        on_device,
        mesh=mesh,
        in_specs=placed,
        out_specs=(
            P("ctx", "head"),
            P("head", "ctx"),
            P("head", "ctx"),
            P("ctx", "head"),
            P("ctx", "head"),
            P("head"),
        ),
        check_vma=False,
    )
```

```python
import functools

import jax
import jax.numpy as jnp
from jax import lax
from jax.experimental import pallas as pl
from jax.experimental.pallas import tpu as pltpu
from jax.sharding import PartitionSpec as P

P_SIZE = 64
N = 128
C = 128
INNER_MARKS = {False: (0.25, 0.4, 0.6, 0.75, 1.0), True: (0.375, 0.5, 0.625, 1.0)}
LOG2E = 1.4426950408889634
F32 = jnp.float32
BF16 = jnp.bfloat16
NT = (((1,), (1,)), ((), ()))
TN = (((0,), (0,)), ((), ()))
NN = (((1,), (0,)), ((), ()))


def dot(a, b, dims):
    return lax.dot_general(a, b, dims, preferred_element_type=F32)


def split(a):
    high = a.astype(BF16)
    return high, (a - high.astype(F32)).astype(BF16)


def halves():
    lane = lax.broadcasted_iota(jnp.int32, (1, 2 * P_SIZE), 1)
    low = (lane < P_SIZE).astype(F32)
    return low, 1.0 - low


def blocks_of(pair):
    low, high = halves()
    return jnp.concatenate([pair * low.astype(pair.dtype), pair * high.astype(pair.dtype)], axis=0)


def params(**more):
    return pltpu.CompilerParams(vmem_limit_bytes=48 * 1024 * 1024, **more)


def prep_kernel(groups, per, decay_ref, step_ref, col_ref, row_ref):
    heads = decay_ref.shape[0]
    lane = lax.broadcasted_iota(jnp.int32, (heads, C), 1)
    for k in range(decay_ref.shape[1] // C):
        at = slice(k * C, (k + 1) * C)
        step = step_ref[:, at]
        cum = decay_ref[:, at]
        shift = 1
        while shift < C:
            cum = cum + jnp.where(lane >= shift, pltpu.roll(cum, shift, 1), 0.0)
            shift *= 2
        total = cum[:, C - 1 :]
        cum2 = cum * LOG2E
        low2 = cum2 - jnp.log(step) * LOG2E
        rise = jnp.exp(cum)
        tail = jnp.exp(total - cum) * step
        for g in range(groups):
            own = slice(g * per, (g + 1) * per)
            pad = jnp.zeros((C - 3 * per, C), F32)
            stacked = jnp.concatenate([low2[own], rise[own], tail[own], pad], axis=0)
            rows = jnp.concatenate([cum2[own], rise[own], tail[own]], axis=0)
            row_ref[g * 3 * per : (g + 1) * 3 * per, at] = rows
            col_ref[at, g * C : (g + 1) * C] = stacked.T


def state_kernel(per, x_ref, dy_ref, k_ref, q_ref, col_ref, tot_ref, pre_ref,
                 h_ref, u_ref, ends_ref, skip_ref, h_s, g_s):
    k = pl.program_id(0)

    @pl.when(k == 0)
    def _():
        h_s[...] = jnp.zeros_like(h_s)
        g_s[...] = jnp.zeros_like(g_s)
        skip_ref[...] = jnp.zeros_like(skip_ref)

    low, _ = halves()
    keys = jnp.concatenate([k_ref[...]] * 2, axis=0)
    queries = jnp.concatenate([q_ref[...]] * 2, axis=0)
    col = col_ref[...]

    def scaled(ref, first):
        parts = []
        for j in range(per // 2):
            a = first + 2 * j
            factor = jnp.where(low > 0, col[:, a : a + 1], col[:, a + 1 : a + 2])
            parts.append(ref[:, 128 * j : 128 * (j + 1)].astype(F32) * factor)
        return jnp.concatenate(split(jnp.concatenate(parts, axis=1)), axis=0)

    h_ref[0] = h_s[...]
    h_s[...] = tot_ref[0] * h_s[...] + dot(keys, scaled(x_ref, 2 * per), TN)
    pull = dot(queries, scaled(dy_ref, per), TN)
    u_ref[0] = pull
    g_s[...] = g_s[...] + pre_ref[0] * pull
    both = x_ref[...].astype(F32) * dy_ref[...].astype(F32)
    skip_ref[...] = skip_ref[...] + jnp.sum(both, axis=0, keepdims=True)

    @pl.when(k == pl.num_programs(0) - 1)
    def _():
        ends_ref[0] = h_s[...]
        ends_ref[1] = g_s[...]


def inner_kernel(per, carried, x_ref, dy_ref, k_ref, q_ref, col_ref, row_ref, *rest):
    z_ref, gq_ref, gk_ref, rc_ref, c_s = rest[carried:]
    mask = lax.broadcasted_iota(jnp.int32, (C, C), 1) >= lax.broadcasted_iota(jnp.int32, (C, C), 0)
    keys = k_ref[...]
    queries = q_ref[...]
    scores = dot(keys, queries, NT)
    total = jnp.zeros((C, C), F32)
    for j in range(per // 2):
        at = slice(128 * j, 128 * (j + 1))
        ups = blocks_of(dy_ref[:, at])
        met = dot(x_ref[:, at], ups, NT)
        highs, lows = [], []
        for i in range(2):
            a = 2 * j + i
            spread = jnp.where(mask, row_ref[a : a + 1, :] - col_ref[:, a : a + 1], -1e4)
            decay = jnp.exp2(spread)
            lm = decay * met[:, i * C : (i + 1) * C]
            total = total + lm
            both = lm * scores
            rc_ref[a : a + 1, :] = jnp.sum(both, axis=0, keepdims=True)
            c_s[:, a : a + 1] = jnp.sum(both, axis=1, keepdims=True)
            high, rest_of = split(decay * scores)
            highs.append(high)
            lows.append(rest_of)
        z_ref[:, at] = dot(jnp.concatenate(highs, axis=1), ups, NN) + dot(
            jnp.concatenate(lows, axis=1), ups, NN
        )
    high, rest_of = split(total)
    gq_ref[...] = dot(high, keys, TN) + dot(rest_of, keys, TN)
    gk_ref[...] = dot(high, queries, NN) + dot(rest_of, queries, NN)
    rc_ref[per:, :] = c_s[...].T[:per]


def outer_kernel(per, nx, carried, x_ref, dy_ref, k_ref, q_ref, col_ref, row_ref, step_ref, h_ref, u_ref,
                 tot_ref, pre_ref, gain_ref, z_ref, gq_ref, gk_ref, rc_ref, *rest):
    got = rest[:nx]
    gx_ref, gstep_ref, gdecay_ref, gkey_ref, gquery_ref, e_s, g_s, r_s, c_s, edge_s = rest[nx + carried :]
    place = lax.rem(lax.axis_index("ctx"), nx)

    @pl.when(pl.program_id(0) == 0)
    def _():
        size = N // nx
        for r in range(nx):
            part = pl.ds(pl.multiple_of(lax.rem(place - r + nx, nx) * size, size), size)
            e_s[part, :] = got[r][0]
            g_s[part, :] = got[r][1]

    low, high_half = halves()
    keys2 = jnp.concatenate([k_ref[...]] * 2, axis=1)
    keys_t = k_ref[...].astype(F32).T
    queries_t = q_ref[...].astype(F32).T
    gq = jnp.zeros((N, C), F32)
    gk = jnp.zeros((N, C), F32)
    for j in range(per // 2):
        at = slice(128 * j, 128 * (j + 1))
        x = x_ref[:, at]
        dy = dy_ref[:, at]
        pull = g_s[:, at]
        tot = tot_ref[0, :, at]
        state = h_ref[0, :, at] + pre_ref[0, :, at] * e_s[:, at]
        g_s[:, at] = tot * pull + u_ref[0, :, at]
        edge = jnp.sum(state * pull, axis=0, keepdims=True) * tot
        s_high, s_low = split(state)
        p_high, p_low = split(pull)
        s_both = jnp.concatenate([blocks_of(s_high), blocks_of(s_low)], axis=1)
        p_both = jnp.concatenate([blocks_of(p_high), blocks_of(p_low)], axis=1)
        to_q = dot(s_both, jnp.concatenate([dy, dy], axis=1), NT)
        to_k = dot(p_both, jnp.concatenate([x, x], axis=1), NT)
        z_out = dot(keys2, jnp.concatenate([p_high, p_low], axis=0), NN)
        a = 2 * j
        tails = [col_ref[:, 2 * per + a + i : 2 * per + a + i + 1] for i in range(2)]
        z = z_ref[:, at] + z_out * jnp.where(low > 0, tails[0], tails[1])
        gx_ref[:, at] = (z + gain_ref[0, :, at] * dy.astype(F32)).astype(BF16)
        for i, half in enumerate((low, high_half)):
            own_q = to_q[i * N : (i + 1) * N] * row_ref[per + a + i : per + a + i + 1, :]
            own_k = to_k[i * N : (i + 1) * N] * row_ref[2 * per + a + i : 2 * per + a + i + 1, :]
            gq = gq + own_q
            gk = gk + own_k
            r_s[a + i : a + i + 1, :] = jnp.sum(own_q * queries_t, axis=0, keepdims=True)
            c_s[a + i : a + i + 1, :] = jnp.sum(own_k * keys_t, axis=0, keepdims=True)
            edge_s[a + i : a + i + 1, :] = edge * half
    gquery_ref[...] = (gq_ref[...] + gq.T).astype(BF16)
    gkey_ref[...] = (gk_ref[...] + gk.T).astype(BF16)
    cols = rc_ref[per:, :] + c_s[...]
    part = rc_ref[:per, :] + r_s[...] - cols
    edge_sum = jnp.sum(edge_s[...] + c_s[...], axis=1, keepdims=True)
    lane = lax.broadcasted_iota(jnp.int32, (per, C), 1)
    part = jnp.where(lane == C - 1, part + edge_sum, part)
    shift = 1
    while shift < C:
        part = part + jnp.where(lane < C - shift, pltpu.roll(part, C - shift, 1), 0.0)
        shift *= 2
    gdecay_ref[...] = part
    gstep_ref[...] = cols / step_ref[...]


def exchange(parts, nx, x, nz):
    kept = lax.dynamic_index_in_dim(parts, x, 1, False)
    got = [kept]
    for r in range(1, nx):
        pairs = [(c * nx + i, c * nx + (i + r) % nx) for c in range(nz) for i in range(nx)]
        sent = lax.dynamic_index_in_dim(parts, (x + r) % nx, 1, False)
        got.append(lax.ppermute(sent, "ctx", pairs))
    return got


def by_sender(got, nx, x):
    out = []
    for j in range(nx):
        one = got[0]
        for r in range(1, nx):
            one = jnp.where((x - j) % nx == r, got[r], one)
        out.append(one)
    return out


def carry_steps(ends, fades, nx, nz, x):
    _, rows, wide = ends.shape
    got = yield exchange(ends.reshape(2, nx, rows // nx, wide), nx, x, nz)
    row_fade = fades()
    all_fade = functools.reduce(lambda a, b: a * b, row_fade)
    both = by_sender(got, nx, x)
    states, pulls = [b[0] for b in both], [b[1] for b in both]
    state_sum = states[0]
    for i in range(1, nx):
        state_sum = row_fade[i] * state_sum + states[i]
    pull_sum = pulls[nx - 1]
    for i in range(nx - 2, -1, -1):
        pull_sum = row_fade[i] * pull_sum + pulls[i]
    entering, leaving, up_send, down_send = None, None, state_sum, pull_sum
    for hop in range(nz - 1):
        up = [(hop * nx + i, (hop + 1) * nx + i) for i in range(nx)]
        down = [((nz - 1 - hop) * nx + i, (nz - 2 - hop) * nx + i) for i in range(nx)]
        came = yield (lax.ppermute(up_send, "ctx", up), lax.ppermute(down_send, "ctx", down))
        entering = came[0] if hop == 0 else entering + came[0]
        leaving = came[1] if hop == 0 else leaving + came[1]
        up_send = all_fade * entering + state_sum
        down_send = all_fade * leaving + pull_sum
    ins, outs = [entering], [leaving]
    for i in range(nx - 1):
        ins.append(row_fade[i] * ins[-1] + states[i])
    for i in range(nx - 1, 0, -1):
        outs.append(row_fade[i] * outs[-1] + pulls[i])
    yield exchange(jnp.stack([jnp.stack(ins), jnp.stack(outs[::-1])]), nx, x, nz)


def on_device(signal, step_size, log_decay, input_map, output_map, skip_gain, grad_out):
    heads, length = step_size.shape
    groups = input_map.shape[1] // N
    per = heads // groups
    wide = per * P_SIZE
    width = heads * P_SIZE
    nk = length // C

    col, row = pl.pallas_call(
        functools.partial(prep_kernel, groups, per),
        out_shape=(
            jax.ShapeDtypeStruct((length, groups * C), F32),
            jax.ShapeDtypeStruct((3 * heads, length), F32),
        ),
        compiler_params=params(),
        name="prep",
    )(log_decay, step_size)

    sums = jnp.sum(log_decay.reshape(heads, nk, C), axis=-1)
    after = lax.broadcasted_iota(jnp.int32, (nk, nk), 0) < lax.broadcasted_iota(jnp.int32, (nk, nk), 1)
    before = jnp.sum(jnp.where(after[None], sums[:, :, None], 0.0), axis=1)
    span = jnp.sum(sums, axis=1)
    chunk_lines = jnp.exp(jnp.concatenate([sums.T, before.T, span[None]], axis=0))
    lines = jnp.concatenate([chunk_lines, skip_gain[None]], axis=0)
    lines = jnp.repeat(lines, P_SIZE, axis=1)[:, None, :]
    fade = lines[2 * nk]

    def spec(shape, index):
        return pl.BlockSpec(shape, index)

    def specs(at):
        return (
            spec((C, wide), lambda g, k: (at(k), g)),
            spec((C, C), lambda g, k: (at(k), g)),
        )

    def fixed(at, g):
        return (
            spec((C, wide), lambda k: (at(k), g)),
            spec((C, C), lambda k: (at(k), g)),
            spec((1, N, wide), lambda k: (at(k), 0, 0)),
            spec((1, 1, wide), lambda k: (at(k), 0, g)),
            spec((1, 1, wide), lambda k: (nk + at(k), 0, g)),
        )

    def state_call(g, row):
        big, small, local, tot, pre = fixed(lambda k: k, g)
        return pl.pallas_call(
            functools.partial(state_kernel, per),
            grid=(nk,),
            in_specs=[big, big, small, small, small, tot, pre],
            out_specs=(local, local, spec((2, N, wide), lambda k: (0, 0, 0)), spec((1, wide), lambda k: (0, 0))),
            out_shape=(
                jax.ShapeDtypeStruct((nk, N, wide), F32),
                jax.ShapeDtypeStruct((nk, N, wide), F32),
                jax.ShapeDtypeStruct((2, N, wide), F32),
                jax.ShapeDtypeStruct((1, wide), F32),
            ),
            scratch_shapes=[pltpu.VMEM((N, wide), F32), pltpu.VMEM((N, wide), F32)],
            compiler_params=params(),
            cost_estimate=pl.CostEstimate(
                flops=8 * length * wide * N, bytes_accessed=12 << 20, transcendentals=0
            ),
            name="states",
        )(signal, grad_out, input_map, output_map, col, lines, lines)

    inner_shapes = (
        jax.ShapeDtypeStruct((length, width), F32),
        jax.ShapeDtypeStruct((length, groups * N), F32),
        jax.ShapeDtypeStruct((length, groups * N), F32),
        jax.ShapeDtypeStruct((2 * heads, length), F32),
    )
    def inner(first, each, carried, row):
        b, s = specs(lambda k: first + k)
        return pl.pallas_call(
            functools.partial(inner_kernel, per, len(carried)),
            grid=(groups, each),
            in_specs=[b, b, s, s, s, spec((3 * per, C), lambda g, k: (g, first + k))]
            + [pl.BlockSpec(memory_space=pltpu.HBM)] * len(carried),
            out_specs=(b, s, s, spec((2 * per, C), lambda g, k: (g, first + k))),
            out_shape=inner_shapes,
            scratch_shapes=[pltpu.VMEM((C, C), F32)],
            input_output_aliases={6 + i: i for i in range(len(carried))},
            compiler_params=params(),
            cost_estimate=pl.CostEstimate(
                flops=8_000_000_000 * each // nk * 4, bytes_accessed=(16 << 20) * each // nk, transcendentals=0
            ),
            name="inner",
        )(signal, grad_out, input_map, output_map, col, row, *carried)

    def outer(g, sums_in, got, work, results):
        def back(k):
            return nk - 1 - k

        big, small, local, tot, pre = fixed(back, g)
        rowed = spec((per, C), lambda k: (g, back(k)))
        operands = [signal, grad_out, input_map, output_map, col, row, step_size, *sums_in,
                    lines, lines, lines, *work, *got]
        return pl.pallas_call(
            functools.partial(outer_kernel, per, nx, len(results)),
            grid=(nk,),
            in_specs=[big, big, small, small, small, spec((3 * per, C), lambda k: (g, back(k))), rowed,
                      local, local, tot, pre, spec((1, 1, wide), lambda k: (2 * nk + 1, 0, g)),
                      big, small, small, spec((2 * per, C), lambda k: (g, back(k)))]
            + [spec((2, N // nx, wide), lambda k: (0, 0, 0))] * nx
            + [pl.BlockSpec(memory_space=pltpu.HBM)] * len(results),
            out_specs=(big, rowed, rowed, small, small),
            out_shape=(
                jax.ShapeDtypeStruct((length, width), BF16),
                jax.ShapeDtypeStruct((heads, length), F32),
                jax.ShapeDtypeStruct((heads, length), F32),
                jax.ShapeDtypeStruct((length, groups * N), BF16),
                jax.ShapeDtypeStruct((length, groups * N), BF16),
            ),
            scratch_shapes=[
                pltpu.VMEM((N, wide), F32),
                pltpu.VMEM((N, wide), F32),
                pltpu.VMEM((per, C), F32),
                pltpu.VMEM((per, C), F32),
                pltpu.VMEM((per, C), F32),
            ],
            input_output_aliases={len(operands) + i: i for i in range(len(results))},
            compiler_params=params(),
            cost_estimate=pl.CostEstimate(
                flops=16 * length * wide * N, bytes_accessed=20 << 20, transcendentals=0
            ),
            name="outer",
        )(*operands, *results)

    count = lax.axis_size("ctx")
    nx = 2 if count < 16 else 4
    nz = count // nx
    place = lax.axis_index("ctx")
    x = place % nx
    marks = [0] + [max(1, round(nk * f)) for f in INNER_MARKS[groups > 1]]
    local, sections, arrived = {}, {}, {}
    skip, strides = None, [1 << i for i in range(count.bit_length() - 1)]
    fades = [fade] + [
        lax.ppermute(fade, "ctx", [(c * nx + i, c * nx + (i + r) % nx) for c in range(nz) for i in range(nx)])
        for r in range(1, nx)
    ]
    fade_rows = []
    work, results = (), ()
    local[0] = state_call(0, row)
    for tick in range(nz + groups + 1):
        sent = {}
        for g in range(groups):
            if tick == g:
                def faded(g=g):
                    return [f[:, g * wide : (g + 1) * wide] for f in fade_rows]

                sections[g] = carry_steps(local[g][2], faded, nx, nz, x)
                sent[g] = next(sections[g])
            elif g < tick <= g + nz:
                sent[g] = sections[g].send(arrived[g])
        moved_skip = ()
        if skip is None and len(local) == groups:
            skip = jnp.concatenate([local[g][3] for g in range(groups)], axis=1)
        if skip is not None and strides:
            stride = strides.pop(0)
            moved_skip = lax.ppermute(skip, "ctx", [(i, i ^ stride) for i in range(count)])
        made = None
        if tick + 1 < groups:
            made = state_call(tick + 1, row)
        elif tick <= nz:
            at = tick - groups + 1
            if marks[at + 1] > marks[at]:
                work = inner(marks[at], marks[at + 1] - marks[at], work, row)
        else:
            g = tick - nz - 1
            results = outer(g, local[g][:2], arrived[g], work, results)
        if tick == nz + groups:
            break
        now_fades = fades if tick == 0 else ()
        sent, moved_skip, made, work, results, row, now_fades = lax.optimization_barrier(
            (sent, moved_skip, made, work, results, row, now_fades)
        )
        arrived.update(sent)
        if tick == 0:
            fade_rows.extend(by_sender(now_fades, nx, x))
        if made is not None:
            local[tick + 1] = made
        if not isinstance(moved_skip, tuple):
            skip = skip + moved_skip
    grad_skip = jnp.sum(skip.reshape(heads, P_SIZE), axis=1)
    return (*results, grad_skip)


def solution(mesh):
    placed = (
        P("ctx", "head"),
        P("head", "ctx"),
        P("head", "ctx"),
        P("ctx", "head"),
        P("ctx", "head"),
        P("head"),
        P("ctx", "head"),
    )
    return jax.shard_map(
        on_device,
        mesh=mesh,
        in_specs=placed,
        out_specs=(
            P("ctx", "head"),
            P("head", "ctx"),
            P("head", "ctx"),
            P("ctx", "head"),
            P("ctx", "head"),
            P("head"),
        ),
        check_vma=False,
    )
```

```python
import functools

import jax
import jax.numpy as jnp
from jax import lax
from jax.experimental import pallas as pl
from jax.experimental.pallas import tpu as pltpu
from jax.sharding import PartitionSpec as P

P_SIZE = 64
N = 128
C = 128
LIMIT = 60 * 1024 * 1024
INNER_MARKS = {False: (0.25, 0.4, 0.6, 0.75, 1.0), True: (0.375, 0.5, 0.625, 1.0)}
LOG2E = 1.4426950408889634
F32 = jnp.float32
BF16 = jnp.bfloat16
NT = (((1,), (1,)), ((), ()))
TN = (((0,), (0,)), ((), ()))
NN = (((1,), (0,)), ((), ()))


def dot(a, b, dims):
    return lax.dot_general(a, b, dims, preferred_element_type=F32)


def split(a):
    high = a.astype(BF16)
    return high, (a - high.astype(F32)).astype(BF16)


def halves():
    lane = lax.broadcasted_iota(jnp.int32, (1, 2 * P_SIZE), 1)
    low = (lane < P_SIZE).astype(F32)
    return low, 1.0 - low


def blocks_of(pair):
    low, high = halves()
    return jnp.concatenate([pair * low.astype(pair.dtype), pair * high.astype(pair.dtype)], axis=0)


def params(**more):
    return pltpu.CompilerParams(vmem_limit_bytes=LIMIT, **more)


def prep_kernel(groups, per, decay_ref, step_ref, col_ref, row_ref):
    heads = decay_ref.shape[0]
    lane = lax.broadcasted_iota(jnp.int32, (heads, C), 1)
    for k in range(decay_ref.shape[1] // C):
        at = slice(k * C, (k + 1) * C)
        step = step_ref[:, at]
        cum = decay_ref[:, at]
        shift = 1
        while shift < C:
            cum = cum + jnp.where(lane >= shift, pltpu.roll(cum, shift, 1), 0.0)
            shift *= 2
        total = cum[:, C - 1 :]
        cum2 = cum * LOG2E
        low2 = cum2 - jnp.log(step) * LOG2E
        rise = jnp.exp(cum)
        tail = jnp.exp(total - cum) * step
        for g in range(groups):
            own = slice(g * per, (g + 1) * per)
            pad = jnp.zeros((C - 3 * per, C), F32)
            stacked = jnp.concatenate([low2[own], rise[own], tail[own], pad], axis=0)
            rows = jnp.concatenate([cum2[own], rise[own], tail[own]], axis=0)
            row_ref[g * 3 * per : (g + 1) * 3 * per, at] = rows
            col_ref[at, g * C : (g + 1) * C] = stacked.T


def state_kernel(per, x_ref, dy_ref, k_ref, q_ref, col_ref, tot_ref, pre_ref,
                 h_ref, u_ref, ends_ref, skip_ref, h_s, g_s, skip_s):
    k = pl.program_id(0)

    @pl.when(k == 0)
    def _():
        h_s[...] = jnp.zeros_like(h_s)
        g_s[...] = jnp.zeros_like(g_s)
        skip_s[...] = jnp.zeros_like(skip_s)

    low, _ = halves()
    keys = jnp.concatenate([k_ref[...]] * 2, axis=0)
    queries = jnp.concatenate([q_ref[...]] * 2, axis=0)
    col = col_ref[...]

    def scaled(ref, first):
        parts = []
        for j in range(per // 2):
            a = first + 2 * j
            factor = jnp.where(low > 0, col[:, a : a + 1], col[:, a + 1 : a + 2])
            parts.append(ref[:, 128 * j : 128 * (j + 1)].astype(F32) * factor)
        return jnp.concatenate(split(jnp.concatenate(parts, axis=1)), axis=0)

    h_ref[0] = h_s[...]
    h_s[...] = tot_ref[0] * h_s[...] + dot(keys, scaled(x_ref, 2 * per), TN)
    pull = dot(queries, scaled(dy_ref, per), TN)
    u_ref[0] = pull
    g_s[...] = g_s[...] + pre_ref[0] * pull
    both = x_ref[...].astype(F32) * dy_ref[...].astype(F32)
    skip_s[...] = skip_s[...] + jnp.sum(both, axis=0, keepdims=True)

    @pl.when(k == pl.num_programs(0) - 1)
    def _():
        ends_ref[0] = h_s[...]
        ends_ref[1] = g_s[...]
        lane = lax.broadcasted_iota(jnp.int32, (1, C), 1)
        line = jnp.zeros((1, C), F32)
        for j in range(per // 2):
            pair = skip_s[:, 128 * j : 128 * (j + 1)]
            for i, half in enumerate(halves()):
                line = jnp.where(lane == 2 * j + i, jnp.sum(pair * half, axis=1, keepdims=True), line)
        skip_ref[...] = line


def inner_kernel(per, carried, x_ref, dy_ref, k_ref, q_ref, col_ref, row_ref, *rest):
    z_ref, gq_ref, gk_ref, rc_ref, c_s = rest[carried:]
    mask = lax.broadcasted_iota(jnp.int32, (C, C), 1) >= lax.broadcasted_iota(jnp.int32, (C, C), 0)
    keys = k_ref[...]
    queries = q_ref[...]
    scores = dot(keys, queries, NT)
    total = jnp.zeros((C, C), F32)
    for j in range(per // 2):
        at = slice(128 * j, 128 * (j + 1))
        ups = blocks_of(dy_ref[:, at])
        met = dot(x_ref[:, at], ups, NT)
        highs, lows = [], []
        for i in range(2):
            a = 2 * j + i
            spread = jnp.where(mask, row_ref[a : a + 1, :] - col_ref[:, a : a + 1], -1e4)
            decay = jnp.exp2(spread)
            lm = decay * met[:, i * C : (i + 1) * C]
            total = total + lm
            both = lm * scores
            rc_ref[a : a + 1, :] = jnp.sum(both, axis=0, keepdims=True)
            c_s[:, a : a + 1] = jnp.sum(both, axis=1, keepdims=True)
            high, rest_of = split(decay * scores)
            highs.append(high)
            lows.append(rest_of)
        z_ref[:, at] = dot(jnp.concatenate(highs, axis=1), ups, NN) + dot(
            jnp.concatenate(lows, axis=1), ups, NN
        )
    high, rest_of = split(total)
    gq_ref[...] = dot(high, keys, TN) + dot(rest_of, keys, TN)
    gk_ref[...] = dot(high, queries, NN) + dot(rest_of, queries, NN)
    rc_ref[per:, :] = c_s[...].T[:per]


def outer_kernel(per, nx, carried, x_ref, dy_ref, k_ref, q_ref, col_ref, row_ref, step_ref, h_ref, u_ref,
                 tot_ref, pre_ref, gain_ref, z_ref, gq_ref, gk_ref, rc_ref, *rest):
    got = rest[:nx]
    gx_ref, gstep_ref, gdecay_ref, gkey_ref, gquery_ref, e_s, g_s, r_s, c_s, edge_s = rest[nx + carried :]
    place = lax.rem(lax.axis_index("ctx"), nx)

    @pl.when(pl.program_id(0) == 0)
    def _():
        size = N // nx
        for r in range(nx):
            part = pl.ds(pl.multiple_of(lax.rem(place - r + nx, nx) * size, size), size)
            e_s[part, :] = got[r][0]
            g_s[part, :] = got[r][1]

    low, high_half = halves()
    keys2 = jnp.concatenate([k_ref[...]] * 2, axis=1)
    keys_t = k_ref[...].astype(F32).T
    queries_t = q_ref[...].astype(F32).T
    gq = jnp.zeros((N, C), F32)
    gk = jnp.zeros((N, C), F32)
    for j in range(per // 2):
        at = slice(128 * j, 128 * (j + 1))
        x = x_ref[:, at]
        dy = dy_ref[:, at]
        pull = g_s[:, at]
        tot = tot_ref[0, :, at]
        state = h_ref[0, :, at] + pre_ref[0, :, at] * e_s[:, at]
        g_s[:, at] = tot * pull + u_ref[0, :, at]
        edge = jnp.sum(state * pull, axis=0, keepdims=True) * tot
        s_high, s_low = split(state)
        p_high, p_low = split(pull)
        s_both = jnp.concatenate([blocks_of(s_high), blocks_of(s_low)], axis=1)
        p_both = jnp.concatenate([blocks_of(p_high), blocks_of(p_low)], axis=1)
        to_q = dot(s_both, jnp.concatenate([dy, dy], axis=1), NT)
        to_k = dot(p_both, jnp.concatenate([x, x], axis=1), NT)
        z_out = dot(keys2, jnp.concatenate([p_high, p_low], axis=0), NN)
        a = 2 * j
        tails = [col_ref[:, 2 * per + a + i : 2 * per + a + i + 1] for i in range(2)]
        z = z_ref[:, at] + z_out * jnp.where(low > 0, tails[0], tails[1])
        gx_ref[:, at] = (z + gain_ref[0, :, at] * dy.astype(F32)).astype(BF16)
        for i, half in enumerate((low, high_half)):
            own_q = to_q[i * N : (i + 1) * N] * row_ref[per + a + i : per + a + i + 1, :]
            own_k = to_k[i * N : (i + 1) * N] * row_ref[2 * per + a + i : 2 * per + a + i + 1, :]
            gq = gq + own_q
            gk = gk + own_k
            r_s[a + i : a + i + 1, :] = jnp.sum(own_q * queries_t, axis=0, keepdims=True)
            c_s[a + i : a + i + 1, :] = jnp.sum(own_k * keys_t, axis=0, keepdims=True)
            edge_s[a + i : a + i + 1, :] = edge * half
    gquery_ref[...] = (gq_ref[...] + gq.T).astype(BF16)
    gkey_ref[...] = (gk_ref[...] + gk.T).astype(BF16)
    cols = rc_ref[per:, :] + c_s[...]
    part = rc_ref[:per, :] + r_s[...] - cols
    edge_sum = jnp.sum(edge_s[...] + c_s[...], axis=1, keepdims=True)
    lane = lax.broadcasted_iota(jnp.int32, (per, C), 1)
    part = jnp.where(lane == C - 1, part + edge_sum, part)
    shift = 1
    while shift < C:
        part = part + jnp.where(lane < C - shift, pltpu.roll(part, C - shift, 1), 0.0)
        shift *= 2
    gdecay_ref[...] = part
    gstep_ref[...] = cols / step_ref[...]


def exchange(parts, nx, x, nz):
    kept = lax.dynamic_index_in_dim(parts, x, 1, False)
    got = [kept]
    for r in range(1, nx):
        pairs = [(c * nx + i, c * nx + (i + r) % nx) for c in range(nz) for i in range(nx)]
        sent = lax.dynamic_index_in_dim(parts, (x + r) % nx, 1, False)
        got.append(lax.ppermute(sent, "ctx", pairs))
    return got


def by_sender(got, nx, x):
    out = []
    for j in range(nx):
        one = got[0]
        for r in range(1, nx):
            one = jnp.where((x - j) % nx == r, got[r], one)
        out.append(one)
    return out


def carry_steps(ends, fades, nx, nz, x, z):
    _, rows, wide = ends.shape
    got = yield exchange(ends.reshape(2, nx, rows // nx, wide), nx, x, nz)
    row_fade = fades()
    all_fade = functools.reduce(lambda a, b: a * b, row_fade)
    both = by_sender(got, nx, x)
    states, pulls = [b[0] for b in both], [b[1] for b in both]
    state_sum = states[0]
    for i in range(1, nx):
        state_sum = row_fade[i] * state_sum + states[i]
    pull_sum = pulls[nx - 1]
    for i in range(nx - 2, -1, -1):
        pull_sum = row_fade[i] * pull_sum + pulls[i]
    entering, leaving, up_send, down_send = jnp.zeros_like(state_sum), jnp.zeros_like(pull_sum), state_sum, pull_sum
    for hop in range(nz - 1):
        down_row = nz - 1 - hop
        pairs = [(hop * nx + i, (hop + 1) * nx + i) for i in range(nx)]
        pairs += [(down_row * nx + i, (down_row - 1) * nx + i) for i in range(nx)]
        came = yield lax.ppermute(jnp.where(z == hop, up_send, down_send), "ctx", pairs)
        entering = jnp.where(z == hop + 1, came, entering)
        leaving = jnp.where(z == down_row - 1, came, leaving)
        up_send = all_fade * entering + state_sum
        down_send = all_fade * leaving + pull_sum
    ins, outs = [entering], [leaving]
    for i in range(nx - 1):
        ins.append(row_fade[i] * ins[-1] + states[i])
    for i in range(nx - 1, 0, -1):
        outs.append(row_fade[i] * outs[-1] + pulls[i])
    yield exchange(jnp.stack([jnp.stack(ins), jnp.stack(outs[::-1])]), nx, x, nz)


def on_device(signal, step_size, log_decay, input_map, output_map, skip_gain, grad_out):
    heads, length = step_size.shape
    groups = input_map.shape[1] // N
    per = heads // groups
    wide = per * P_SIZE
    width = heads * P_SIZE
    nk = length // C

    col, row = pl.pallas_call(
        functools.partial(prep_kernel, groups, per),
        out_shape=(
            jax.ShapeDtypeStruct((length, groups * C), F32),
            jax.ShapeDtypeStruct((3 * heads, length), F32),
        ),
        compiler_params=params(),
        name="prep",
    )(log_decay, step_size)

    sums = jnp.sum(log_decay.reshape(heads, nk, C), axis=-1)
    after = lax.broadcasted_iota(jnp.int32, (nk, nk), 0) < lax.broadcasted_iota(jnp.int32, (nk, nk), 1)
    before = jnp.sum(jnp.where(after[None], sums[:, :, None], 0.0), axis=1)
    span = jnp.sum(sums, axis=1)
    chunk_lines = jnp.exp(jnp.concatenate([sums.T, before.T, span[None]], axis=0))
    lines = jnp.concatenate([chunk_lines, skip_gain[None]], axis=0)
    lines = jnp.repeat(lines, P_SIZE, axis=1)[:, None, :]
    fade = lines[2 * nk]

    def spec(shape, index):
        return pl.BlockSpec(shape, index)

    def specs(at):
        return (
            spec((C, wide), lambda g, k: (at(k), g)),
            spec((C, C), lambda g, k: (at(k), g)),
        )

    def fixed(at, g):
        return (
            spec((C, wide), lambda k: (at(k), g)),
            spec((C, C), lambda k: (at(k), g)),
            spec((1, N, wide), lambda k: (at(k), 0, 0)),
            spec((1, 1, wide), lambda k: (at(k), 0, g)),
            spec((1, 1, wide), lambda k: (nk + at(k), 0, g)),
        )

    def state_call(g, row):
        big, small, local, tot, pre = fixed(lambda k: k, g)
        return pl.pallas_call(
            functools.partial(state_kernel, per),
            grid=(nk,),
            in_specs=[big, big, small, small, small, tot, pre],
            out_specs=(local, local, spec((2, N, wide), lambda k: (0, 0, 0)), spec((1, C), lambda k: (0, 0))),
            out_shape=(
                jax.ShapeDtypeStruct((nk, N, wide), F32),
                jax.ShapeDtypeStruct((nk, N, wide), F32),
                jax.ShapeDtypeStruct((2, N, wide), F32),
                jax.ShapeDtypeStruct((1, C), F32),
            ),
            scratch_shapes=[pltpu.VMEM((N, wide), F32), pltpu.VMEM((N, wide), F32), pltpu.VMEM((1, wide), F32)],
            compiler_params=params(),
            cost_estimate=pl.CostEstimate(
                flops=8 * length * wide * N, bytes_accessed=12 << 20, transcendentals=0
            ),
            name="states",
        )(signal, grad_out, input_map, output_map, col, lines, lines)

    inner_shapes = (
        jax.ShapeDtypeStruct((length, width), F32),
        jax.ShapeDtypeStruct((length, groups * N), F32),
        jax.ShapeDtypeStruct((length, groups * N), F32),
        jax.ShapeDtypeStruct((2 * heads, length), F32),
    )
    def inner(first, each, carried, row):
        b, s = specs(lambda k: first + k)
        return pl.pallas_call(
            functools.partial(inner_kernel, per, len(carried)),
            grid=(groups, each),
            in_specs=[b, b, s, s, s, spec((3 * per, C), lambda g, k: (g, first + k))]
            + [pl.BlockSpec(memory_space=pltpu.HBM)] * len(carried),
            out_specs=(b, s, s, spec((2 * per, C), lambda g, k: (g, first + k))),
            out_shape=inner_shapes,
            scratch_shapes=[pltpu.VMEM((C, C), F32)],
            input_output_aliases={6 + i: i for i in range(len(carried))},
            compiler_params=params(),
            cost_estimate=pl.CostEstimate(
                flops=8_000_000_000 * each // nk * 4, bytes_accessed=(16 << 20) * each // nk, transcendentals=0
            ),
            name="inner",
        )(signal, grad_out, input_map, output_map, col, row, *carried)

    def outer(g, sums_in, got, work, results):
        def back(k):
            return nk - 1 - k

        big, small, local, tot, pre = fixed(back, g)
        rowed = spec((per, C), lambda k: (g, back(k)))
        operands = [signal, grad_out, input_map, output_map, col, row, step_size, *sums_in,
                    lines, lines, lines, *work, *got]
        return pl.pallas_call(
            functools.partial(outer_kernel, per, nx, len(results)),
            grid=(nk,),
            in_specs=[big, big, small, small, small, spec((3 * per, C), lambda k: (g, back(k))), rowed,
                      local, local, tot, pre, spec((1, 1, wide), lambda k: (2 * nk + 1, 0, g)),
                      big, small, small, spec((2 * per, C), lambda k: (g, back(k)))]
            + [spec((2, N // nx, wide), lambda k: (0, 0, 0))] * nx
            + [pl.BlockSpec(memory_space=pltpu.HBM)] * len(results),
            out_specs=(big, rowed, rowed, small, small),
            out_shape=(
                jax.ShapeDtypeStruct((length, width), BF16),
                jax.ShapeDtypeStruct((heads, length), F32),
                jax.ShapeDtypeStruct((heads, length), F32),
                jax.ShapeDtypeStruct((length, groups * N), BF16),
                jax.ShapeDtypeStruct((length, groups * N), BF16),
            ),
            scratch_shapes=[
                pltpu.VMEM((N, wide), F32),
                pltpu.VMEM((N, wide), F32),
                pltpu.VMEM((per, C), F32),
                pltpu.VMEM((per, C), F32),
                pltpu.VMEM((per, C), F32),
            ],
            input_output_aliases={len(operands) + i: i for i in range(len(results))},
            compiler_params=params(),
            cost_estimate=pl.CostEstimate(
                flops=16 * length * wide * N, bytes_accessed=20 << 20, transcendentals=0
            ),
            name="outer",
        )(*operands, *results)

    count = lax.axis_size("ctx")
    nx = 2 if count < 16 else 4
    nz = count // nx
    place = lax.axis_index("ctx")
    x, z = place % nx, place // nx
    marks = [0] + [max(1, round(nk * f)) for f in INNER_MARKS[groups > 1]]
    local, sections, arrived = {}, {}, {}
    skip, strides = None, [1 << i for i in range(count.bit_length() - 1)]
    fades = [fade] + [
        lax.ppermute(fade, "ctx", [(c * nx + i, c * nx + (i + r) % nx) for c in range(nz) for i in range(nx)])
        for r in range(1, nx)
    ]
    fade_rows = []
    work, results = (), ()
    local[0] = state_call(0, row)
    for tick in range(nz + groups + 1):
        sent = {}
        for g in range(groups):
            if tick == g:
                def faded(g=g):
                    return [f[:, g * wide : (g + 1) * wide] for f in fade_rows]

                sections[g] = carry_steps(local[g][2], faded, nx, nz, x, z)
                sent[g] = next(sections[g])
            elif g < tick <= g + nz:
                sent[g] = sections[g].send(arrived[g])
        moved_skip = ()
        if skip is None and len(local) == groups:
            skip = jnp.concatenate([local[g][3] for g in range(groups)], axis=1)
        if skip is not None and strides:
            stride = strides.pop(0)
            moved_skip = lax.ppermute(skip, "ctx", [(i, i ^ stride) for i in range(count)])
        made = None
        if tick + 1 < groups:
            made = state_call(tick + 1, row)
        elif tick <= nz:
            at = tick - groups + 1
            if marks[at + 1] > marks[at]:
                work = inner(marks[at], marks[at + 1] - marks[at], work, row)
        else:
            g = tick - nz - 1
            results = outer(g, local[g][:2], arrived[g], work, results)
        if tick == nz + groups:
            break
        now_fades = fades if tick == 0 else ()
        sent, moved_skip, made, work, results, row, now_fades = lax.optimization_barrier(
            (sent, moved_skip, made, work, results, row, now_fades)
        )
        arrived.update(sent)
        if tick == 0:
            fade_rows.extend(by_sender(now_fades, nx, x))
        if made is not None:
            local[tick + 1] = made
        if not isinstance(moved_skip, tuple):
            skip = skip + moved_skip
    grad_skip = skip.reshape(groups, C)[:, :per].reshape(heads)
    return (*results, grad_skip)


def solution(mesh):
    placed = (
        P("ctx", "head"),
        P("head", "ctx"),
        P("head", "ctx"),
        P("ctx", "head"),
        P("ctx", "head"),
        P("head"),
        P("ctx", "head"),
    )
    return jax.shard_map(
        on_device,
        mesh=mesh,
        in_specs=placed,
        out_specs=(
            P("ctx", "head"),
            P("head", "ctx"),
            P("head", "ctx"),
            P("ctx", "head"),
            P("ctx", "head"),
            P("head"),
        ),
        check_vma=False,
    )
```
